32 devices in a mesh: ctx: 16 (over z, x, core), head: 2 (over y).
Axes of the slice: x: 2, y: 2, z: 4, core: 2. Of those that a mesh axis runs over, the one named last changes fastest.
Arguments:
- tokens: bfloat16 [4096, 4096], P('ctx', 'head'), may hold values from -26 to 26
- w_query: bfloat16 [4096, 2048], P('ctx', 'head'), may hold values from -0.09375 to 0.09375, as said below
- w_key: bfloat16 [4096, 2048], P('ctx', 'head'), may hold values from -1.5 to 1.5
- w_value: bfloat16 [4096, 2048], P('ctx', 'head'), may hold values from -0.09375 to 0.09375
- w_out: bfloat16 [2048, 4096], P('head', 'ctx'), may hold values from -0.125 to 0.125
- query_down: bfloat16 [4096, 8], replicated, may hold values from -0.09375 to 0.09375
- query_up: bfloat16 [8, 2048], P(None, 'head'), may hold values from -0.5 to 0.5
- value_down: bfloat16 [4096, 8], replicated, may hold values from -0.09375 to 0.09375
- value_up: bfloat16 [8, 2048], P(None, 'head'), may hold values from -0.5 to 0.5
- shifted: int32 [16], replicated, may hold values from 0 to 1, as said below
- grad_out: bfloat16 [4096, 4096], P('ctx', 'head'), may hold values from -6 to 6
Outputs:
- output: bfloat16 [4096, 4096], P('ctx', 'head')
- grad_tokens: bfloat16 [4096, 4096], P('ctx', 'head')
- grad_query_down: float32 [4096, 8], replicated
- grad_query_up: float32 [8, 2048], P(None, 'head')
- grad_value_down: float32 [4096, 8], replicated
- grad_value_up: float32 [8, 2048], P(None, 'head')
The draws below stay inside these ranges and needn't reach their ends.
Inputs may be any that keep to these rules, and one draw needn't show every extreme that they name: Exactly 8 of the heads are shifted. `w_query`: entries within 6 / sqrt(4096).
All inputs are finite; a program needn't handle non-finite values.
Results may differ from the reference program's by a relative error of at most 0.0095.
The reference program's roundings to bfloat16 on the way (of `normed`, `low_q`, `query`, `prob`, `context`, `d_context`, `dscore` and `dq_pre`) count: a program that leaves them out, or rounds other values in their place, can miss the bound.
Values may be sent and summed in bfloat16 or wider, within the bound.
A program may use at most 192 MiB of HBM per device.

```python
import math
import jax
import jax.numpy as jnp
from jax import lax

D = 4096
HEADS = 16
HEAD_DIM = 128
RANK = 8
HD = 2048
SEQ = 4096
GROUP = 2048
SHIFT = 1024


def shared_base(key):
    return jnp.clip(jax.random.normal(key, (D, HD), jnp.float32), -6.0, 6.0)


def draw_w_query(key, part):
    base = shared_base(key)
    return (base * D ** (-0.5)).astype(jnp.bfloat16)


def draw_w_key(key, part):
    key = jax.random.fold_in(key, 12)
    first = jax.random.fold_in(key, 0)
    result = jnp.clip(jax.random.normal(first, (D, HD), jnp.float32), -6.0, 6.0) * D ** (-0.5)
    return result.astype(jnp.bfloat16)


def draw_tokens(key, part):
    key = jax.random.fold_in(key, 14)
    first, second = jax.random.split(key)
    ramp = jnp.arange(D, dtype=jnp.float32) / (D - 1)
    rough = jnp.exp(jax.random.uniform(second, (D,), jnp.float32, math.log(0.7), math.log(1.4)))
    column = 0.3 * jnp.exp(ramp * math.log(10.0)) * rough
    values = jnp.clip(jax.random.normal(first, (SEQ, D), jnp.float32), -6.0, 6.0)
    return (values * column[None, :]).astype(jnp.bfloat16)


def draw_shifted(key, part):
    key = jax.random.fold_in(key, 13)
    order = jax.random.permutation(key, HEADS)
    return (order < HEADS // 2).astype(jnp.int32)


def shard_levels(rng, dims, shards, smallest, top_value):
    loudness = 1.0
    for position, shards_of in shards:
        steps = jax.random.uniform(jax.random.fold_in(jax.random.fold_in(rng, 6), position), (shards_of,), jnp.float32, smallest / len(shards), top_value / len(shards))
        loudness = loudness * jnp.repeat(jnp.exp(steps), dims[position] // shards_of).reshape((-1,) + (1,) * (len(dims) - 1 - position))
    return loudness


def centred(rng, dims, deviation, limit, cuts=(), held_as=jnp.bfloat16):
    values = jax.random.normal(rng, dims, jnp.float32) * deviation
    if len(cuts) > 0:
        values = shard_levels(rng, dims, cuts, -0.22, 0.18) * values
    return jnp.clip(values, min=-limit, max=limit).astype(held_as)


def setup_inputs(seed: int = 0) -> dict:
    seeds = jax.random.split(jax.random.key(seed), 12)
    tokens = draw_tokens(jax.random.fold_in(seeds[11], 71), 0)
    w_query = draw_w_query(jax.random.fold_in(seeds[11], 71), 0)
    w_key = draw_w_key(jax.random.fold_in(seeds[11], 71), 0)
    w_value = centred(seeds[3], (D, HD), D ** -0.5, 0.09375, ((0, 16), (1, 2)))
    w_out = centred(seeds[4], (HD, D), HD ** -0.5, 0.125, ((0, 2), (1, 16)))
    query_down = centred(seeds[5], (D, RANK), D ** -0.5, 0.09375)
    query_up = centred(seeds[6], (RANK, HD), (RANK * 16) ** -0.5, 0.5, ((1, 2),))
    value_down = centred(seeds[7], (D, RANK), D ** -0.5, 0.09375)
    value_up = centred(seeds[8], (RANK, HD), (RANK * 16) ** -0.5, 0.5, ((1, 2),))
    shifted = draw_shifted(jax.random.fold_in(seeds[11], 71), 0)
    grad_out = centred(seeds[10], (SEQ, D), 1.0, 6.0, ((0, 16), (1, 2)))
    return dict(tokens=tokens, w_query=w_query, w_key=w_key, w_value=w_value, w_out=w_out, query_down=query_down, query_up=query_up, value_down=value_down, value_up=value_up, shifted=shifted, grad_out=grad_out)


def rope(values, positions, sign):
    count = values.shape[0]
    shaped = values.reshape(count, values.shape[1] // HEAD_DIM, HEAD_DIM)
    half = HEAD_DIM // 2
    freq = jnp.power(10000.0, -jnp.arange(half, dtype=jnp.float32) * 2.0 / HEAD_DIM)
    angle = positions.astype(jnp.float32)[:, None] * freq[None, :]
    cosine = jnp.cos(angle)[:, None, :]
    sine = sign * jnp.sin(angle)[:, None, :]
    first = shaped[:, :, :half]
    second = shaped[:, :, half:]
    rotated = jnp.concatenate([first * cosine - second * sine, second * cosine + first * sine], axis=2)
    return rotated.reshape(count, values.shape[1])

def head_pass(packed):
    query, key, value, d_context, offset = packed
    groups = SEQ // GROUP
    scale = 1.0 / HEAD_DIM ** 0.5

    def rolled(array):
        return jnp.roll(array, -offset, axis=0).reshape(groups, GROUP, HEAD_DIM).astype(jnp.float32)
    query_r = rolled(query)
    key_r = rolled(key)
    value_r = rolled(value)
    dctx_r = rolled(d_context)
    scores = jnp.einsum('gqd,gkd->gqk', query_r, key_r) * scale
    allowed = jnp.tril(jnp.ones((GROUP, GROUP), dtype=bool))[None]
    scores = jnp.where(allowed, scores, -jnp.inf)
    top = lax.optimization_barrier(jnp.max(scores, axis=-1, keepdims=True))
    expo = jnp.exp(scores - top)
    prob32 = expo / lax.optimization_barrier(jnp.sum(expo, axis=-1, keepdims=True))
    prob = prob32.astype(jnp.bfloat16)
    context = jnp.einsum('gqk,gkd->gqd', prob.astype(jnp.float32), value_r).astype(jnp.bfloat16)
    dprob = jnp.einsum('gqd,gkd->gqk', dctx_r, value_r)
    delta = lax.optimization_barrier(jnp.sum(prob32 * dprob, axis=-1, keepdims=True))
    dscore = (prob32 * (dprob - delta) * scale).astype(jnp.bfloat16).astype(jnp.float32)
    grad_q = jnp.einsum('gqk,gkd->gqd', dscore, key_r)
    grad_k = jnp.einsum('gqk,gqd->gkd', dscore, query_r)
    grad_v = jnp.einsum('gqk,gqd->gkd', prob.astype(jnp.float32), dctx_r)

    def back(array):
        return jnp.roll(array.reshape(SEQ, HEAD_DIM), offset, axis=0)
    return (back(context), back(grad_q), back(grad_k), back(grad_v))

def reference(tokens, w_query, w_key, w_value, w_out, query_down, query_up, value_down, value_up, shifted, grad_out):
    tokens32 = tokens.astype(jnp.float32)
    rinv = lax.rsqrt(lax.optimization_barrier(jnp.mean(tokens32 * tokens32, axis=-1, keepdims=True)) + 1e-05)
    xn = tokens32 * rinv
    normed = xn.astype(jnp.bfloat16)
    low_q = jnp.dot(normed, query_down, preferred_element_type=jnp.float32).astype(jnp.bfloat16)
    low_v = jnp.dot(normed, value_down, preferred_element_type=jnp.float32).astype(jnp.bfloat16)
    positions = jnp.arange(SEQ, dtype=jnp.int32)
    q_lin = jnp.dot(normed, w_query, preferred_element_type=jnp.float32) + 2.0 * jnp.dot(low_q, query_up, preferred_element_type=jnp.float32)
    query = rope(q_lin, positions, 1.0).astype(jnp.bfloat16)
    key = rope(jnp.dot(normed, w_key, preferred_element_type=jnp.float32), positions, 1.0).astype(jnp.bfloat16)
    value = (jnp.dot(normed, w_value, preferred_element_type=jnp.float32) + 2.0 * jnp.dot(low_v, value_up, preferred_element_type=jnp.float32)).astype(jnp.bfloat16)
    d_context = jnp.dot(grad_out, w_out.T, preferred_element_type=jnp.float32).astype(jnp.bfloat16)

    def split(array):
        return array.reshape(SEQ, HEADS, HEAD_DIM).transpose(1, 0, 2)

    def merge(array):
        return array.transpose(1, 0, 2).reshape(SEQ, HD)
    offsets = (shifted * SHIFT).astype(jnp.int32)
    context, grad_q, grad_k, grad_v = lax.map(head_pass, (split(query), split(key), split(value), split(d_context), offsets))
    attn = jnp.dot(merge(context), w_out, preferred_element_type=jnp.float32)
    output = (tokens32 + attn).astype(jnp.bfloat16)
    dq_pre = rope(merge(grad_q), positions, -1.0).astype(jnp.bfloat16)
    dk_pre = rope(merge(grad_k), positions, -1.0).astype(jnp.bfloat16)
    dv_b = merge(grad_v).astype(jnp.bfloat16)
    g_q = jnp.dot(dq_pre, query_up.T, preferred_element_type=jnp.float32)
    g_v = jnp.dot(dv_b, value_up.T, preferred_element_type=jnp.float32)
    d_normed = jnp.dot(dq_pre, w_query.T, preferred_element_type=jnp.float32)
    d_normed = d_normed + jnp.dot(dk_pre, w_key.T, preferred_element_type=jnp.float32)
    d_normed = d_normed + jnp.dot(dv_b, w_value.T, preferred_element_type=jnp.float32)
    d_normed = d_normed + 2.0 * jnp.dot(g_q, query_down.astype(jnp.float32).T, precision=lax.Precision.HIGHEST)
    d_normed = d_normed + 2.0 * jnp.dot(g_v, value_down.astype(jnp.float32).T, precision=lax.Precision.HIGHEST)
    row_mean = lax.optimization_barrier(jnp.sum(d_normed * xn, axis=-1, keepdims=True)) / D
    grad_tokens = (grad_out.astype(jnp.float32) + rinv * (d_normed - xn * row_mean)).astype(jnp.bfloat16)
    scale_out = 1.0 / SEQ ** 0.5
    normed32 = normed.astype(jnp.float32)
    grad_query_down = 2.0 * jnp.dot(normed32.T, g_q, precision=lax.Precision.HIGHEST) * scale_out
    grad_value_down = 2.0 * jnp.dot(normed32.T, g_v, precision=lax.Precision.HIGHEST) * scale_out
    grad_query_up = 2.0 * jnp.dot(low_q.T, dq_pre, preferred_element_type=jnp.float32) * scale_out
    grad_value_up = 2.0 * jnp.dot(low_v.T, dv_b, preferred_element_type=jnp.float32) * scale_out
    return (output, grad_tokens, grad_query_down, grad_query_up, grad_value_down, grad_value_up)
```

```python
import functools

import jax
import jax.numpy as jnp
from jax import lax
from jax.experimental import pallas as pl
from jax.experimental.pallas import tpu as pltpu
from jax.sharding import PartitionSpec as P

HEAD_DIM = 128
G_BLOCKS = 8
LAST = (((1,), (1,)), ((), ()))
FIRST = (((0,), (0,)), ((), ()))


def angles(positions):
    half = HEAD_DIM // 2
    freq = jnp.power(10000.0, -jnp.arange(half, dtype=jnp.float32) * 2.0 / HEAD_DIM)
    angle = positions.astype(jnp.float32)[:, None] * freq[None, :]
    return jnp.cos(angle), jnp.sin(angle)


def rope(values, cosine, sine):
    count = values.shape[0]
    shaped = values.reshape(count, values.shape[1] // HEAD_DIM, HEAD_DIM)
    half = HEAD_DIM // 2
    cosine = cosine[:, None, :]
    sine = sine[:, None, :]
    first = shaped[:, :, :half]
    second = shaped[:, :, half:]
    rotated = jnp.concatenate(
        [first * cosine - second * sine, second * cosine + first * sine], axis=2
    )
    return rotated.reshape(count, values.shape[1])


def swapped(value):
    return lax.ppermute(value, "head", [(0, 1), (1, 0)])


def gather_head(value):
    if lax.axis_size("head") != 2:
        return lax.all_gather(value, "head", axis=1, tiled=True)
    other = swapped(value)
    first = lax.axis_index("head") == 0
    left = jnp.where(first, value, other)
    right = jnp.where(first, other, value)
    return jnp.concatenate([left, right], axis=1)


def scatter_head(value):
    if lax.axis_size("head") != 2:
        return lax.psum_scatter(value, "head", scatter_dimension=1, tiled=True)
    place = lax.axis_index("head")
    width = value.shape[1] // 2
    theirs = lax.dynamic_slice_in_dim(value, (1 - place) * width, width, 1)
    mine = lax.dynamic_slice_in_dim(value, place * width, width, 1)
    return mine + swapped(theirs.astype(jnp.bfloat16)).astype(jnp.float32)


def sum_head(value):
    if lax.axis_size("head") != 2:
        return lax.psum(value, "head")
    return value + swapped(value)


def attend_kernel(block, q_ref, k_ref, v_ref, g_ref, cos_ref, sin_ref, out_ref, dk_acc, dv_acc):
    count = q_ref.shape[0]
    scale = 1.0 / HEAD_DIM**0.5
    dk_acc[...] = jnp.zeros_like(dk_acc)
    dv_acc[...] = jnp.zeros_like(dv_acc)

    def unrope(values, rows):
        turned = pltpu.roll(values, HEAD_DIM // 2, 1)
        return (values * cos_ref[rows, :] + turned * sin_ref[rows, :]).astype(jnp.bfloat16)

    for step in range(count // block):
        rows = slice(step * block, (step + 1) * block)
        seen = slice(0, (step + 1) * block)
        q = q_ref[rows, :]
        g = g_ref[rows, :]
        k = k_ref[seen, :]
        v = v_ref[seen, :]
        scores = lax.dot_general(q, k, LAST, preferred_element_type=jnp.float32) * scale
        q_place = step * block + lax.broadcasted_iota(jnp.int32, scores.shape, 0)
        k_place = lax.broadcasted_iota(jnp.int32, scores.shape, 1)
        scores = jnp.where(k_place <= q_place, scores, -jnp.inf)
        expo = jnp.exp(scores - jnp.max(scores, axis=-1, keepdims=True))
        prob32 = expo * (1.0 / jnp.sum(expo, axis=-1, keepdims=True))
        prob = prob32.astype(jnp.bfloat16)
        out_ref[0, rows, :] = jnp.dot(prob, v, preferred_element_type=jnp.float32).astype(
            jnp.bfloat16
        )
        dprob = lax.dot_general(g, v, LAST, preferred_element_type=jnp.float32)
        delta = jnp.sum(prob32 * dprob, axis=-1, keepdims=True)
        dscore = (prob32 * (dprob - delta) * scale).astype(jnp.bfloat16)
        out_ref[1, rows, :] = unrope(jnp.dot(dscore, k, preferred_element_type=jnp.float32), rows)
        dk_acc[seen, :] += lax.dot_general(dscore, q, FIRST, preferred_element_type=jnp.float32)
        dv_acc[seen, :] += lax.dot_general(prob, g, FIRST, preferred_element_type=jnp.float32)
    out_ref[2, :, :] = unrope(dk_acc[...], slice(0, count))
    out_ref[3, :, :] = dv_acc[...].astype(jnp.bfloat16)


def attend(query, key, value, d_context, cosine, sine):
    count = query.shape[0]
    return pl.pallas_call(
        functools.partial(attend_kernel, 256),
        out_shape=jax.ShapeDtypeStruct((4, count, HEAD_DIM), jnp.bfloat16),
        in_specs=[pl.BlockSpec(memory_space=pltpu.VMEM)] * 6,
        out_specs=pl.BlockSpec(memory_space=pltpu.VMEM),
        scratch_shapes=[
            pltpu.VMEM((count, HEAD_DIM), jnp.float32),
            pltpu.VMEM((count, HEAD_DIM), jnp.float32),
        ],
        compiler_params=pltpu.CompilerParams(vmem_limit_bytes=48 * 1024 * 1024),
        cost_estimate=pl.CostEstimate(
            flops=10 * count * count * HEAD_DIM // 2,
            bytes_accessed=16 * count * HEAD_DIM * 2,
            transcendentals=count * count // 2,
        ),
    )(query, key, value, d_context, cosine, sine)


def per_device(
    tokens,
    w_query,
    w_key,
    w_value,
    w_out,
    query_down,
    query_up,
    value_down,
    value_up,
    shifted,
    grad_out,
):
    rows = tokens.shape[0]
    slice_width = tokens.shape[1]
    ctx_count = lax.axis_size("ctx")
    ctx_place = lax.axis_index("ctx")
    head_count = lax.axis_size("head")
    head_place = lax.axis_index("head")
    width_local = w_query.shape[1]
    heads_local = width_local // HEAD_DIM
    seq_total = ctx_count * rows
    group = G_BLOCKS * rows
    groups = ctx_count // G_BLOCKS
    items = heads_local * groups
    assert items <= ctx_count
    half_group = G_BLOCKS // 2
    rank = query_down.shape[1]

    whole = [
        lax.all_gather(w, "ctx", axis=0, tiled=True) for w in (w_query, w_key, w_value, w_out.T)
    ]

    full_x = gather_head(tokens)
    full_dy = gather_head(grad_out)
    full32 = full_x.astype(jnp.float32)
    rinv = lax.rsqrt(jnp.mean(full32 * full32, axis=-1, keepdims=True) + 1e-05)
    xn = full32 * rinv
    normed = xn.astype(jnp.bfloat16)
    low_q = jnp.dot(normed, query_down, preferred_element_type=jnp.float32).astype(jnp.bfloat16)
    low_v = jnp.dot(normed, value_down, preferred_element_type=jnp.float32).astype(jnp.bfloat16)
    positions = ctx_place * rows + jnp.arange(rows, dtype=jnp.int32)
    cosine, sine = angles(positions)
    q_lin = jnp.dot(normed, whole[0], preferred_element_type=jnp.float32)
    k_lin = jnp.dot(normed, whole[1], preferred_element_type=jnp.float32)
    v_lin = jnp.dot(normed, whole[2], preferred_element_type=jnp.float32)
    query = rope(
        q_lin + 2.0 * jnp.dot(low_q, query_up, preferred_element_type=jnp.float32), cosine, sine
    ).astype(jnp.bfloat16)
    key = rope(k_lin, cosine, sine).astype(jnp.bfloat16)
    value = (v_lin + 2.0 * jnp.dot(low_v, value_up, preferred_element_type=jnp.float32)).astype(
        jnp.bfloat16
    )
    d_context = jnp.dot(full_dy, whole[3], preferred_element_type=jnp.float32).astype(jnp.bfloat16)

    local_shift = lax.dynamic_slice_in_dim(shifted, head_place * heads_local, heads_local)
    item = jnp.minimum(ctx_place, items - 1)
    item_group = item % groups
    item_shift = lax.dynamic_index_in_dim(local_shift, item // groups, keepdims=False)
    start = (item_group * G_BLOCKS + item_shift * half_group) % ctx_count

    packed = jnp.stack([query, key, value, d_context])
    packed = packed.reshape(4, rows, heads_local, HEAD_DIM).transpose(2, 0, 1, 3)
    packed = jnp.broadcast_to(
        packed[:, None], (heads_local, groups, 4, rows, HEAD_DIM)
    ).reshape(items, 4, rows, HEAD_DIM)
    if items < ctx_count:
        packed = jnp.pad(packed, ((0, ctx_count - items), (0, 0), (0, 0), (0, 0)))
    arrived = lax.all_to_all(packed, "ctx", 0, 0, tiled=True)
    arrived = jnp.concatenate([arrived, arrived[:G_BLOCKS]], axis=0)
    mine = lax.dynamic_slice_in_dim(arrived, start, G_BLOCKS, 0)
    mine = mine.transpose(1, 0, 2, 3).reshape(4, group, HEAD_DIM)

    item_pos = (start * rows + jnp.arange(group, dtype=jnp.int32)) % seq_total
    item_cos, item_sin = angles(item_pos)
    item_cos = jnp.concatenate([item_cos, item_cos], axis=1)
    item_sin = jnp.concatenate([item_sin, -item_sin], axis=1)
    results = attend(mine[0], mine[1], mine[2], mine[3], item_cos, item_sin)

    results = results.reshape(4, G_BLOCKS, rows, HEAD_DIM).transpose(1, 0, 2, 3)
    back = jnp.concatenate([results] * (ctx_count // G_BLOCKS), axis=0)
    back = jnp.concatenate([back, back], axis=0)
    back = lax.dynamic_slice_in_dim(back, (ctx_count - start) % ctx_count, ctx_count, 0)
    returned = lax.all_to_all(back, "ctx", 0, 0, tiled=True)
    returned = returned[:items].reshape(heads_local, groups, 4, rows, HEAD_DIM)
    my_group = ((ctx_place - local_shift * half_group) % ctx_count) // G_BLOCKS
    chosen = returned[:, 0]
    for other in range(1, groups):
        chosen = jnp.where((my_group == other)[:, None, None, None], returned[:, other], chosen)
    chosen = chosen.transpose(1, 2, 0, 3).reshape(4, rows, width_local)
    context, dq_pre, dk_pre, dv_b = chosen[0], chosen[1], chosen[2], chosen[3]

    partial_value = lax.dot_general(context, whole[3], LAST, preferred_element_type=jnp.float32)
    output = (tokens.astype(jnp.float32) + scatter_head(partial_value)).astype(jnp.bfloat16)

    g_q = jnp.dot(dq_pre, query_up.T, preferred_element_type=jnp.float32)
    g_v = jnp.dot(dv_b, value_up.T, preferred_element_type=jnp.float32)
    g_both = 2.0 * jnp.concatenate([g_q, g_v], axis=1)
    downs = jnp.concatenate([query_down, value_down], axis=1).astype(jnp.float32)
    d_normed = lax.dot_general(dq_pre, whole[0], LAST, preferred_element_type=jnp.float32)
    d_normed += lax.dot_general(dk_pre, whole[1], LAST, preferred_element_type=jnp.float32)
    d_normed += lax.dot_general(dv_b, whole[2], LAST, preferred_element_type=jnp.float32)
    d_normed += lax.dot_general(g_both, downs, LAST, precision=lax.Precision.HIGHEST)
    row_mean = sum_head(jnp.sum(d_normed * xn, axis=-1, keepdims=True)) / full_x.shape[1]
    x_slice = tokens.astype(jnp.float32) * rinv
    grad_tokens = (
        grad_out.astype(jnp.float32) + rinv * (scatter_head(d_normed) - x_slice * row_mean)
    ).astype(jnp.bfloat16)

    scale_out = 1.0 / seq_total**0.5
    down = lax.dot_general(
        g_both, normed.astype(jnp.float32), FIRST, precision=lax.Precision.HIGHEST
    )
    up_q = 2.0 * lax.dot_general(low_q, dq_pre, FIRST, preferred_element_type=jnp.float32)
    up_v = 2.0 * lax.dot_general(low_v, dv_b, FIRST, preferred_element_type=jnp.float32)
    ups = jnp.concatenate([up_q, up_v], axis=0)
    wide = jnp.zeros((2 * rank, head_count * width_local), jnp.float32)
    wide = lax.dynamic_update_slice_in_dim(wide, ups, head_place * width_local, 1)
    total = lax.psum(jnp.concatenate([down, wide], axis=1), ("ctx", "head")) * scale_out
    depth = full_x.shape[1]
    downs_out = total[:, :depth].T
    ups_out = lax.dynamic_slice_in_dim(total, depth + head_place * width_local, width_local, 1)
    return (
        output,
        grad_tokens,
        downs_out[:, :rank],
        ups_out[:rank],
        downs_out[:, rank:],
        ups_out[rank:],
    )


def solution(mesh):
    in_specs = (
        P("ctx", "head"),
        P("ctx", "head"),
        P("ctx", "head"),
        P("ctx", "head"),
        P("head", "ctx"),
        P(),
        P(None, "head"),
        P(),
        P(None, "head"),
        P(),
        P("ctx", "head"),
    )
    out_specs = (P("ctx", "head"), P("ctx", "head"), P(), P(None, "head"), P(), P(None, "head"))
    return jax.shard_map(
        per_device, mesh=mesh, in_specs=in_specs, out_specs=out_specs, check_vma=False
    )
```

```python
import functools

import jax
import jax.numpy as jnp
from jax import lax
from jax.experimental import pallas as pl
from jax.experimental.pallas import tpu as pltpu
from jax.sharding import PartitionSpec as P

HEAD_DIM = 128
G_BLOCKS = 8
LAST = (((1,), (1,)), ((), ()))
FIRST = (((0,), (0,)), ((), ()))


def angles(positions):
    half = HEAD_DIM // 2
    freq = jnp.power(10000.0, -jnp.arange(half, dtype=jnp.float32) * 2.0 / HEAD_DIM)
    angle = positions.astype(jnp.float32)[:, None] * freq[None, :]
    return jnp.cos(angle), jnp.sin(angle)


def rope(values, cosine, sine):
    count = values.shape[0]
    shaped = values.reshape(count, values.shape[1] // HEAD_DIM, HEAD_DIM)
    half = HEAD_DIM // 2
    cosine = cosine[:, None, :]
    sine = sine[:, None, :]
    first = shaped[:, :, :half]
    second = shaped[:, :, half:]
    rotated = jnp.concatenate(
        [first * cosine - second * sine, second * cosine + first * sine], axis=2
    )
    return rotated.reshape(count, values.shape[1])


def swapped(value):
    return lax.ppermute(value, "head", [(0, 1), (1, 0)])


def gather_head(value):
    if lax.axis_size("head") != 2:
        return lax.all_gather(value, "head", axis=1, tiled=True)
    other = swapped(value)
    first = lax.axis_index("head") == 0
    left = jnp.where(first, value, other)
    right = jnp.where(first, other, value)
    return jnp.concatenate([left, right], axis=1)


def scatter_head(value):
    if lax.axis_size("head") != 2:
        return lax.psum_scatter(value, "head", scatter_dimension=1, tiled=True)
    place = lax.axis_index("head")
    width = value.shape[1] // 2
    theirs = lax.dynamic_slice_in_dim(value, (1 - place) * width, width, 1)
    mine = lax.dynamic_slice_in_dim(value, place * width, width, 1)
    return mine + swapped(theirs.astype(jnp.bfloat16)).astype(jnp.float32)


def sum_head(value):
    if lax.axis_size("head") != 2:
        return lax.psum(value, "head")
    return value + swapped(value)


def attend_kernel(block, q_ref, k_ref, v_ref, g_ref, cos_ref, sin_ref, out_ref, dk_acc, dv_acc):
    count = q_ref.shape[0]
    scale = 1.0 / HEAD_DIM**0.5
    dk_acc[...] = jnp.zeros_like(dk_acc)
    dv_acc[...] = jnp.zeros_like(dv_acc)

    def unrope(values, rows):
        turned = pltpu.roll(values, HEAD_DIM // 2, 1)
        return (values * cos_ref[rows, :] + turned * sin_ref[rows, :]).astype(jnp.bfloat16)

    for step in range(count // block):
        rows = slice(step * block, (step + 1) * block)
        seen = slice(0, (step + 1) * block)
        q = q_ref[rows, :]
        g = g_ref[rows, :]
        k = k_ref[seen, :]
        v = v_ref[seen, :]
        scores = lax.dot_general(q, k, LAST, preferred_element_type=jnp.float32) * scale
        q_place = step * block + lax.broadcasted_iota(jnp.int32, scores.shape, 0)
        k_place = lax.broadcasted_iota(jnp.int32, scores.shape, 1)
        scores = jnp.where(k_place <= q_place, scores, -jnp.inf)
        expo = jnp.exp(scores - jnp.max(scores, axis=-1, keepdims=True))
        prob32 = expo * (1.0 / jnp.sum(expo, axis=-1, keepdims=True))
        prob = prob32.astype(jnp.bfloat16)
        out_ref[0, rows, :] = jnp.dot(prob, v, preferred_element_type=jnp.float32).astype(
            jnp.bfloat16
        )
        dprob = lax.dot_general(g, v, LAST, preferred_element_type=jnp.float32)
        delta = jnp.sum(prob32 * dprob, axis=-1, keepdims=True)
        dscore = (prob32 * (dprob - delta) * scale).astype(jnp.bfloat16)
        out_ref[1, rows, :] = unrope(jnp.dot(dscore, k, preferred_element_type=jnp.float32), rows)
        dk_acc[seen, :] += lax.dot_general(dscore, q, FIRST, preferred_element_type=jnp.float32)
        dv_acc[seen, :] += lax.dot_general(prob, g, FIRST, preferred_element_type=jnp.float32)
    out_ref[2, :, :] = unrope(dk_acc[...], slice(0, count))
    out_ref[3, :, :] = dv_acc[...].astype(jnp.bfloat16)


def attend(query, key, value, d_context, cosine, sine):
    count = query.shape[0]
    return pl.pallas_call(
        functools.partial(attend_kernel, 256),
        out_shape=jax.ShapeDtypeStruct((4, count, HEAD_DIM), jnp.bfloat16),
        in_specs=[pl.BlockSpec(memory_space=pltpu.VMEM)] * 6,
        out_specs=pl.BlockSpec(memory_space=pltpu.VMEM),
        scratch_shapes=[
            pltpu.VMEM((count, HEAD_DIM), jnp.float32),
            pltpu.VMEM((count, HEAD_DIM), jnp.float32),
        ],
        compiler_params=pltpu.CompilerParams(vmem_limit_bytes=48 * 1024 * 1024),
        cost_estimate=pl.CostEstimate(
            flops=10 * count * count * HEAD_DIM // 2,
            bytes_accessed=16 * count * HEAD_DIM * 2,
            transcendentals=count * count // 2,
        ),
    )(query, key, value, d_context, cosine, sine)


def rolled(value, begin):
    count = value.shape[0]
    return lax.dynamic_slice_in_dim(jnp.concatenate([value, value], axis=0), begin, count, 0)


def spread_pairs(packed, turn, item_cos, item_sin):
    heads, _, rows, _ = packed.shape
    count = lax.axis_size("ctx")
    core = lax.axis_index("ctx") % 2
    even = core == 0
    pairs = [(place, place ^ 1) for place in range(count)]

    def swap(low, high):
        kept = jnp.where(even, low, high)
        return kept, lax.ppermute(jnp.where(even, high, low), "ctx", pairs)

    arrived = lax.all_to_all(packed.reshape(count, 2, rows, HEAD_DIM), "ctx", 0, 0, tiled=True)
    arrived = rolled(arrived, turn)
    kept, other = swap(arrived[:G_BLOCKS], arrived[G_BLOCKS:])

    def flat(array):
        return array.transpose(1, 0, 2, 3).reshape(2, G_BLOCKS * rows, HEAD_DIM)

    kept, other = flat(kept), flat(other)
    low = jnp.where(even, kept, other)
    high = jnp.where(even, other, kept)
    results = attend(low[0], low[1], high[0], high[1], item_cos, item_sin)
    results = results.reshape(4, G_BLOCKS, rows, HEAD_DIM).transpose(1, 0, 2, 3)
    kept, other = swap(results[:, :2], results[:, 2:])
    both = jnp.concatenate([jnp.where(even, kept, other), jnp.where(even, other, kept)], axis=0)
    returned = lax.all_to_all(rolled(both, (count - turn) % count), "ctx", 0, 0, tiled=True)
    return returned.reshape(heads, 4, rows, HEAD_DIM)


def spread_copies(packed, local_shift, start, items, item_cos, item_sin):
    heads, _, rows, _ = packed.shape
    count = lax.axis_size("ctx")
    groups = items // heads
    packed = jnp.broadcast_to(packed[:, None], (heads, groups, 4, rows, HEAD_DIM))
    packed = packed.reshape(items, 4, rows, HEAD_DIM)
    if items < count:
        packed = jnp.pad(packed, ((0, count - items), (0, 0), (0, 0), (0, 0)))
    arrived = lax.all_to_all(packed, "ctx", 0, 0, tiled=True)
    mine = rolled(arrived, start)[:G_BLOCKS]
    mine = mine.transpose(1, 0, 2, 3).reshape(4, G_BLOCKS * rows, HEAD_DIM)
    results = attend(mine[0], mine[1], mine[2], mine[3], item_cos, item_sin)
    results = results.reshape(4, G_BLOCKS, rows, HEAD_DIM).transpose(1, 0, 2, 3)
    back = rolled(jnp.concatenate([results] * (count // G_BLOCKS), axis=0), (count - start) % count)
    returned = lax.all_to_all(back, "ctx", 0, 0, tiled=True)
    returned = returned[:items].reshape(heads, groups, 4, rows, HEAD_DIM)
    turn = local_shift * (G_BLOCKS // 2)
    my_group = ((lax.axis_index("ctx") - turn) % count) // G_BLOCKS
    chosen = returned[:, 0]
    for other in range(1, groups):
        chosen = jnp.where((my_group == other)[:, None, None, None], returned[:, other], chosen)
    return chosen


def sum_ctx(value):
    count = lax.axis_size("ctx")
    if value.size % (count * 128) != 0:
        return lax.psum(value, "ctx")
    parts = value.reshape(count, value.size // (count * 128), 128)
    part = jnp.sum(lax.all_to_all(parts, "ctx", 0, 0, tiled=True), axis=0, keepdims=True)
    whole = lax.all_to_all(jnp.broadcast_to(part, parts.shape), "ctx", 0, 0, tiled=True)
    return whole.reshape(value.shape)


def per_device(
    tokens,
    w_query,
    w_key,
    w_value,
    w_out,
    query_down,
    query_up,
    value_down,
    value_up,
    shifted,
    grad_out,
):
    rows = tokens.shape[0]
    slice_width = tokens.shape[1]
    ctx_count = lax.axis_size("ctx")
    ctx_place = lax.axis_index("ctx")
    head_place = lax.axis_index("head")
    width_local = w_query.shape[1]
    heads_local = width_local // HEAD_DIM
    seq_total = ctx_count * rows
    group = G_BLOCKS * rows
    groups = ctx_count // G_BLOCKS
    items = heads_local * groups
    assert items <= ctx_count
    half_group = G_BLOCKS // 2
    rank = query_down.shape[1]

    weights = lax.all_gather(
        jnp.concatenate([w_query, w_key, w_value, w_out.T], axis=1), "ctx", axis=0, tiled=True
    )
    w_qkv = weights[:, : 3 * width_local]
    w_out_t = weights[:, 3 * width_local :]

    full_x = gather_head(tokens)
    full_dy = gather_head(grad_out)
    full32 = full_x.astype(jnp.float32)
    rinv = lax.rsqrt(jnp.mean(full32 * full32, axis=-1, keepdims=True) + 1e-05)
    xn = full32 * rinv
    normed = xn.astype(jnp.bfloat16)
    low_q = jnp.dot(normed, query_down, preferred_element_type=jnp.float32).astype(jnp.bfloat16)
    low_v = jnp.dot(normed, value_down, preferred_element_type=jnp.float32).astype(jnp.bfloat16)
    positions = ctx_place * rows + jnp.arange(rows, dtype=jnp.int32)
    cosine, sine = angles(positions)
    linear = jnp.dot(normed, w_qkv, preferred_element_type=jnp.float32)
    q_lin, k_lin, v_lin = jnp.split(linear, 3, axis=1)
    query = rope(
        q_lin + 2.0 * jnp.dot(low_q, query_up, preferred_element_type=jnp.float32), cosine, sine
    ).astype(jnp.bfloat16)
    key = rope(k_lin, cosine, sine).astype(jnp.bfloat16)
    value = (v_lin + 2.0 * jnp.dot(low_v, value_up, preferred_element_type=jnp.float32)).astype(
        jnp.bfloat16
    )
    d_context = jnp.dot(full_dy, w_out_t, preferred_element_type=jnp.float32).astype(jnp.bfloat16)

    local_shift = lax.dynamic_slice_in_dim(shifted, head_place * heads_local, heads_local)
    item = jnp.minimum(ctx_place, items - 1)
    item_shift = lax.dynamic_index_in_dim(local_shift, item // groups, keepdims=False)
    start = (item % groups * G_BLOCKS + item_shift * half_group) % ctx_count
    item_pos = (start * rows + jnp.arange(group, dtype=jnp.int32)) % seq_total
    item_cos, item_sin = angles(item_pos)
    item_cos = jnp.concatenate([item_cos, item_cos], axis=1)
    item_sin = jnp.concatenate([item_sin, -item_sin], axis=1)

    packed = jnp.stack([query, key, value, d_context])
    packed = packed.reshape(4, rows, heads_local, HEAD_DIM).transpose(2, 0, 1, 3)
    if groups == 2 and items == ctx_count:
        chosen = spread_pairs(packed, item_shift * half_group, item_cos, item_sin)
    else:
        chosen = spread_copies(packed, local_shift, start, items, item_cos, item_sin)
    chosen = chosen.transpose(1, 2, 0, 3).reshape(4, rows, width_local)
    context, dq_pre, dk_pre, dv_b = chosen[0], chosen[1], chosen[2], chosen[3]

    partial_value = lax.dot_general(context, w_out_t, LAST, preferred_element_type=jnp.float32)
    output = (tokens.astype(jnp.float32) + scatter_head(partial_value)).astype(jnp.bfloat16)

    g_q = jnp.dot(dq_pre, query_up.T, preferred_element_type=jnp.float32)
    g_v = jnp.dot(dv_b, value_up.T, preferred_element_type=jnp.float32)
    g_both = 2.0 * jnp.concatenate([g_q, g_v], axis=1)
    downs = jnp.concatenate([query_down, value_down], axis=1).astype(jnp.float32)
    grads = jnp.concatenate([dq_pre, dk_pre, dv_b], axis=1)
    d_normed = lax.dot_general(grads, w_qkv, LAST, preferred_element_type=jnp.float32)
    d_normed += lax.dot_general(g_both, downs, LAST, precision=lax.Precision.HIGHEST)
    row_mean = sum_head(jnp.sum(d_normed * xn, axis=-1, keepdims=True)) / full_x.shape[1]
    x_slice = tokens.astype(jnp.float32) * rinv
    grad_tokens = (
        grad_out.astype(jnp.float32) + rinv * (scatter_head(d_normed) - x_slice * row_mean)
    ).astype(jnp.bfloat16)

    scale_out = 1.0 / seq_total**0.5
    down = lax.dot_general(
        g_both, normed.astype(jnp.float32), FIRST, precision=lax.Precision.HIGHEST
    )
    up_q = 2.0 * lax.dot_general(low_q, dq_pre, FIRST, preferred_element_type=jnp.float32)
    up_v = 2.0 * lax.dot_general(low_v, dv_b, FIRST, preferred_element_type=jnp.float32)
    ups = jnp.concatenate([up_q, up_v], axis=0)
    total = sum_ctx(jnp.concatenate([sum_head(down), ups], axis=1)) * scale_out
    depth = full_x.shape[1]
    downs_out = total[:, :depth].T
    ups_out = total[:, depth:]
    return (
        output,
        grad_tokens,
        downs_out[:, :rank],
        ups_out[:rank],
        downs_out[:, rank:],
        ups_out[rank:],
    )


def solution(mesh):
    in_specs = (
        P("ctx", "head"),
        P("ctx", "head"),
        P("ctx", "head"),
        P("ctx", "head"),
        P("head", "ctx"),
        P(),
        P(None, "head"),
        P(),
        P(None, "head"),
        P(),
        P("ctx", "head"),
    )
    out_specs = (P("ctx", "head"), P("ctx", "head"), P(), P(None, "head"), P(), P(None, "head"))
    return jax.shard_map(
        per_device, mesh=mesh, in_specs=in_specs, out_specs=out_specs, check_vma=False
    )
```

```python
import functools

import jax
import jax.numpy as jnp
from jax import lax
from jax.experimental import pallas as pl
from jax.experimental.pallas import tpu as pltpu
from jax.sharding import PartitionSpec as P

HEAD_DIM = 128
G_BLOCKS = 8
LAST = (((1,), (1,)), ((), ()))
FIRST = (((0,), (0,)), ((), ()))


def angles(positions):
    half = HEAD_DIM // 2
    freq = jnp.power(10000.0, -jnp.arange(half, dtype=jnp.float32) * 2.0 / HEAD_DIM)
    angle = positions.astype(jnp.float32)[:, None] * freq[None, :]
    return jnp.cos(angle), jnp.sin(angle)


def rope(values, cosine, sine):
    count = values.shape[0]
    shaped = values.reshape(count, values.shape[1] // HEAD_DIM, HEAD_DIM)
    half = HEAD_DIM // 2
    cosine = cosine[:, None, :]
    sine = sine[:, None, :]
    first = shaped[:, :, :half]
    second = shaped[:, :, half:]
    rotated = jnp.concatenate(
        [first * cosine - second * sine, second * cosine + first * sine], axis=2
    )
    return rotated.reshape(count, values.shape[1])


def swapped(value):
    return lax.ppermute(value, "head", [(0, 1), (1, 0)])


def gather_head(value):
    if lax.axis_size("head") != 2:
        return lax.all_gather(value, "head", axis=1, tiled=True)
    other = swapped(value)
    first = lax.axis_index("head") == 0
    left = jnp.where(first, value, other)
    right = jnp.where(first, other, value)
    return jnp.concatenate([left, right], axis=1)


def scatter_head(value):
    if lax.axis_size("head") != 2:
        return lax.psum_scatter(value, "head", scatter_dimension=1, tiled=True)
    place = lax.axis_index("head")
    width = value.shape[1] // 2
    theirs = lax.dynamic_slice_in_dim(value, (1 - place) * width, width, 1)
    mine = lax.dynamic_slice_in_dim(value, place * width, width, 1)
    return mine + swapped(theirs.astype(jnp.bfloat16)).astype(jnp.float32)


def sum_head(value):
    if lax.axis_size("head") != 2:
        return lax.psum(value, "head")
    return value + swapped(value)


def attend_kernel(block, q_ref, k_ref, v_ref, g_ref, cos_ref, sin_ref, out_ref, dk_acc, dv_acc):
    count = q_ref.shape[0]
    scale = 1.0 / HEAD_DIM**0.5
    dk_acc[...] = jnp.zeros_like(dk_acc)
    dv_acc[...] = jnp.zeros_like(dv_acc)

    def unrope(values, rows):
        turned = pltpu.roll(values, HEAD_DIM // 2, 1)
        return (values * cos_ref[rows, :] + turned * sin_ref[rows, :]).astype(jnp.bfloat16)

    for step in range(count // block):
        rows = slice(step * block, (step + 1) * block)
        seen = slice(0, (step + 1) * block)
        q = q_ref[rows, :]
        g = g_ref[rows, :]
        k = k_ref[seen, :]
        v = v_ref[seen, :]
        scores = lax.dot_general(q, k, LAST, preferred_element_type=jnp.float32) * scale
        q_place = step * block + lax.broadcasted_iota(jnp.int32, scores.shape, 0)
        k_place = lax.broadcasted_iota(jnp.int32, scores.shape, 1)
        scores = jnp.where(k_place <= q_place, scores, -jnp.inf)
        expo = jnp.exp(scores - jnp.max(scores, axis=-1, keepdims=True))
        prob32 = expo * (1.0 / jnp.sum(expo, axis=-1, keepdims=True))
        prob = prob32.astype(jnp.bfloat16)
        out_ref[0, rows, :] = jnp.dot(prob, v, preferred_element_type=jnp.float32).astype(
            jnp.bfloat16
        )
        dprob = lax.dot_general(g, v, LAST, preferred_element_type=jnp.float32)
        delta = jnp.sum(prob32 * dprob, axis=-1, keepdims=True)
        dscore = (prob32 * (dprob - delta) * scale).astype(jnp.bfloat16)
        out_ref[1, rows, :] = unrope(jnp.dot(dscore, k, preferred_element_type=jnp.float32), rows)
        dk_acc[seen, :] += lax.dot_general(dscore, q, FIRST, preferred_element_type=jnp.float32)
        dv_acc[seen, :] += lax.dot_general(prob, g, FIRST, preferred_element_type=jnp.float32)
    out_ref[2, :, :] = unrope(dk_acc[...], slice(0, count))
    out_ref[3, :, :] = dv_acc[...].astype(jnp.bfloat16)


def attend(query, key, value, d_context, cosine, sine):
    count = query.shape[0]
    return pl.pallas_call(
        functools.partial(attend_kernel, 256),
        out_shape=jax.ShapeDtypeStruct((4, count, HEAD_DIM), jnp.bfloat16),
        in_specs=[pl.BlockSpec(memory_space=pltpu.VMEM)] * 6,
        out_specs=pl.BlockSpec(memory_space=pltpu.VMEM),
        scratch_shapes=[
            pltpu.VMEM((count, HEAD_DIM), jnp.float32),
            pltpu.VMEM((count, HEAD_DIM), jnp.float32),
        ],
        compiler_params=pltpu.CompilerParams(vmem_limit_bytes=48 * 1024 * 1024),
        cost_estimate=pl.CostEstimate(
            flops=10 * count * count * HEAD_DIM // 2,
            bytes_accessed=16 * count * HEAD_DIM * 2,
            transcendentals=count * count // 2,
        ),
    )(query, key, value, d_context, cosine, sine)


def rolled(value, begin):
    count = value.shape[0]
    return lax.dynamic_slice_in_dim(jnp.concatenate([value, value], axis=0), begin, count, 0)


def spread_halves(packed, turn, item_cos, item_sin):
    heads, kinds, rows, _ = packed.shape
    count = lax.axis_size("ctx")
    even = lax.axis_index("ctx") % 2 == 0
    pairs = [(place, place ^ 1) for place in range(count)]
    part = rows // 2

    def swap(low, high):
        kept = jnp.where(even, low, high)
        other = lax.ppermute(jnp.where(even, high, low), "ctx", pairs)
        return jnp.where(even, kept, other), jnp.where(even, other, kept)

    packed = packed.reshape(heads, kinds, 2, part, HEAD_DIM).transpose(0, 2, 1, 3, 4)
    packed = packed.reshape(count, kinds, part, HEAD_DIM)
    arrived = rolled(lax.all_to_all(packed, "ctx", 0, 0, tiled=True), turn)
    low, high = swap(arrived[:G_BLOCKS], arrived[G_BLOCKS:])
    mine = jnp.stack([low, high], axis=1).transpose(2, 0, 1, 3, 4)
    mine = mine.reshape(kinds, G_BLOCKS * rows, HEAD_DIM)
    results = attend(mine[0], mine[1], mine[2], mine[3], item_cos, item_sin)
    results = results.reshape(4, G_BLOCKS, 2, part, HEAD_DIM)
    low, high = swap(
        results[:, :, 0].transpose(1, 0, 2, 3), results[:, :, 1].transpose(1, 0, 2, 3)
    )
    both = rolled(jnp.concatenate([low, high], axis=0), (count - turn) % count)
    first, rest = both[:, :1], both[:, 1:]
    first = lax.all_to_all(first, "ctx", 0, 0, tiled=True)
    first, rest = lax.optimization_barrier((first, rest))
    rest = lax.all_to_all(rest, "ctx", 0, 0, tiled=True)

    def merged(array):
        kinds = array.shape[1]
        array = array.reshape(heads, 2, kinds, part, HEAD_DIM).transpose(1, 3, 2, 0, 4)
        return array.reshape(rows, kinds * heads * HEAD_DIM)

    return merged(first), merged(rest)


def spread_copies(packed, local_shift, start, items, item_cos, item_sin):
    heads, _, rows, _ = packed.shape
    count = lax.axis_size("ctx")
    groups = items // heads
    packed = jnp.broadcast_to(packed[:, None], (heads, groups, 4, rows, HEAD_DIM))
    packed = packed.reshape(items, 4, rows, HEAD_DIM)
    if items < count:
        packed = jnp.pad(packed, ((0, count - items), (0, 0), (0, 0), (0, 0)))
    arrived = lax.all_to_all(packed, "ctx", 0, 0, tiled=True)
    mine = rolled(arrived, start)[:G_BLOCKS]
    mine = mine.transpose(1, 0, 2, 3).reshape(4, G_BLOCKS * rows, HEAD_DIM)
    results = attend(mine[0], mine[1], mine[2], mine[3], item_cos, item_sin)
    results = results.reshape(4, G_BLOCKS, rows, HEAD_DIM).transpose(1, 0, 2, 3)
    back = rolled(jnp.concatenate([results] * (count // G_BLOCKS), axis=0), (count - start) % count)
    returned = lax.all_to_all(back, "ctx", 0, 0, tiled=True)
    returned = returned[:items].reshape(heads, groups, 4, rows, HEAD_DIM)
    turn = local_shift * (G_BLOCKS // 2)
    my_group = ((lax.axis_index("ctx") - turn) % count) // G_BLOCKS
    chosen = returned[:, 0]
    for other in range(1, groups):
        chosen = jnp.where((my_group == other)[:, None, None, None], returned[:, other], chosen)
    chosen = chosen.transpose(2, 1, 0, 3).reshape(rows, 4 * heads * HEAD_DIM)
    return chosen[:, : heads * HEAD_DIM], chosen[:, heads * HEAD_DIM :]


def sum_ctx(value):
    count = lax.axis_size("ctx")
    if value.size % (count * 128) != 0:
        return lax.psum(value, "ctx")
    parts = value.reshape(count, value.size // (count * 128), 128)
    part = jnp.sum(lax.all_to_all(parts, "ctx", 0, 0, tiled=True), axis=0, keepdims=True)
    whole = lax.all_to_all(jnp.broadcast_to(part, parts.shape), "ctx", 0, 0, tiled=True)
    return whole.reshape(value.shape)


def per_device(
    tokens,
    w_query,
    w_key,
    w_value,
    w_out,
    query_down,
    query_up,
    value_down,
    value_up,
    shifted,
    grad_out,
):
    rows = tokens.shape[0]
    slice_width = tokens.shape[1]
    ctx_count = lax.axis_size("ctx")
    ctx_place = lax.axis_index("ctx")
    head_place = lax.axis_index("head")
    width_local = w_query.shape[1]
    heads_local = width_local // HEAD_DIM
    seq_total = ctx_count * rows
    group = G_BLOCKS * rows
    groups = ctx_count // G_BLOCKS
    items = heads_local * groups
    assert items <= ctx_count
    half_group = G_BLOCKS // 2
    rank = query_down.shape[1]

    weights = lax.all_gather(
        jnp.concatenate([w_query, w_key, w_value, w_out.T], axis=1), "ctx", axis=0, tiled=True
    )
    w_qkv = weights[:, : 3 * width_local]
    w_out_t = weights[:, 3 * width_local :]

    full_x = gather_head(tokens)
    full_dy = gather_head(grad_out)
    local_shift = lax.dynamic_slice_in_dim(shifted, head_place * heads_local, heads_local)
    item = jnp.minimum(ctx_place, items - 1)
    item_shift = lax.dynamic_index_in_dim(local_shift, item // groups, keepdims=False)
    start = (item % groups * G_BLOCKS + item_shift * half_group) % ctx_count
    item_pos = (start * rows + jnp.arange(group, dtype=jnp.int32)) % seq_total
    item_cos, item_sin = angles(item_pos)
    item_cos = jnp.concatenate([item_cos, item_cos], axis=1)
    item_sin = jnp.concatenate([item_sin, -item_sin], axis=1)
    positions = ctx_place * rows + jnp.arange(rows, dtype=jnp.int32)
    cosine, sine = angles(positions)
    full_x, item_cos, item_sin, cosine, sine = lax.optimization_barrier(
        (full_x, item_cos, item_sin, cosine, sine)
    )
    full32 = full_x.astype(jnp.float32)
    rinv = lax.rsqrt(jnp.mean(full32 * full32, axis=-1, keepdims=True) + 1e-05)
    xn = full32 * rinv
    normed = xn.astype(jnp.bfloat16)
    low_q = jnp.dot(normed, query_down, preferred_element_type=jnp.float32).astype(jnp.bfloat16)
    low_v = jnp.dot(normed, value_down, preferred_element_type=jnp.float32).astype(jnp.bfloat16)
    linear = jnp.dot(normed, w_qkv, preferred_element_type=jnp.float32)
    q_lin, k_lin, v_lin = jnp.split(linear, 3, axis=1)
    query = rope(
        q_lin + 2.0 * jnp.dot(low_q, query_up, preferred_element_type=jnp.float32), cosine, sine
    ).astype(jnp.bfloat16)
    key = rope(k_lin, cosine, sine).astype(jnp.bfloat16)
    value = (v_lin + 2.0 * jnp.dot(low_v, value_up, preferred_element_type=jnp.float32)).astype(
        jnp.bfloat16
    )
    d_context = jnp.dot(full_dy, w_out_t, preferred_element_type=jnp.float32).astype(jnp.bfloat16)

    packed = jnp.stack([query, key, value, d_context])
    packed = packed.reshape(4, rows, heads_local, HEAD_DIM).transpose(2, 0, 1, 3)
    if groups == 2 and items == ctx_count:
        context, grads = spread_halves(packed, item_shift * half_group, item_cos, item_sin)
    else:
        context, grads = spread_copies(packed, local_shift, start, items, item_cos, item_sin)

    partial_value = lax.dot_general(context, w_out_t, LAST, preferred_element_type=jnp.float32)
    output = (tokens.astype(jnp.float32) + scatter_head(partial_value)).astype(jnp.bfloat16)

    scale_out = 1.0 / seq_total**0.5
    dq_pre = grads[:, :width_local]
    dv_b = grads[:, 2 * width_local :]
    g_q = lax.dot_general(query_up, dq_pre, LAST, preferred_element_type=jnp.float32)
    g_v = lax.dot_general(value_up, dv_b, LAST, preferred_element_type=jnp.float32)
    g_both = 2.0 * jnp.concatenate([g_q, g_v], axis=0)
    down = jnp.dot(
        sum_head(g_both), normed.astype(jnp.float32), precision=lax.Precision.HIGHEST
    )
    up_q = 2.0 * lax.dot_general(low_q, dq_pre, FIRST, preferred_element_type=jnp.float32)
    up_v = 2.0 * lax.dot_general(low_v, dv_b, FIRST, preferred_element_type=jnp.float32)
    sums = jnp.concatenate([down, jnp.concatenate([up_q, up_v], axis=0)], axis=1)
    sums, grads = lax.optimization_barrier((sums, grads))
    total = sum_ctx(sums) * scale_out

    downs = jnp.concatenate([query_down, value_down], axis=1).astype(jnp.float32)
    d_normed = lax.dot_general(grads, w_qkv, LAST, preferred_element_type=jnp.float32)
    d_normed += lax.dot_general(
        g_both, downs, (((0,), (1,)), ((), ())), precision=lax.Precision.HIGHEST
    )
    row_mean = sum_head(jnp.sum(d_normed * xn, axis=-1, keepdims=True)) / full_x.shape[1]
    x_slice = tokens.astype(jnp.float32) * rinv
    grad_tokens = (
        grad_out.astype(jnp.float32) + rinv * (scatter_head(d_normed) - x_slice * row_mean)
    ).astype(jnp.bfloat16)

    depth = full_x.shape[1]
    downs_out = total[:, :depth].T
    ups_out = total[:, depth:]
    return (
        output,
        grad_tokens,
        downs_out[:, :rank],
        ups_out[:rank],
        downs_out[:, rank:],
        ups_out[rank:],
    )


def solution(mesh):
    in_specs = (
        P("ctx", "head"),
        P("ctx", "head"),
        P("ctx", "head"),
        P("ctx", "head"),
        P("head", "ctx"),
        P(),
        P(None, "head"),
        P(),
        P(None, "head"),
        P(),
        P("ctx", "head"),
    )
    out_specs = (P("ctx", "head"), P("ctx", "head"), P(), P(None, "head"), P(), P(None, "head"))
    return jax.shard_map(
        per_device, mesh=mesh, in_specs=in_specs, out_specs=out_specs, check_vma=False
    )
```

```python
import functools

import jax
import jax.numpy as jnp
from jax import lax
from jax.experimental import pallas as pl
from jax.experimental.pallas import tpu as pltpu
from jax.sharding import PartitionSpec as P

HEAD_DIM = 128
G_BLOCKS = 8
LAST = (((1,), (1,)), ((), ()))
FIRST = (((0,), (0,)), ((), ()))


def angles(positions):
    half = HEAD_DIM // 2
    freq = jnp.power(10000.0, -jnp.arange(half, dtype=jnp.float32) * 2.0 / HEAD_DIM)
    angle = positions.astype(jnp.float32)[:, None] * freq[None, :]
    return jnp.cos(angle), jnp.sin(angle)


def rope(values, cosine, sine):
    count = values.shape[0]
    shaped = values.reshape(count, values.shape[1] // HEAD_DIM, HEAD_DIM)
    half = HEAD_DIM // 2
    cosine = cosine[:, None, :]
    sine = sine[:, None, :]
    first = shaped[:, :, :half]
    second = shaped[:, :, half:]
    rotated = jnp.concatenate(
        [first * cosine - second * sine, second * cosine + first * sine], axis=2
    )
    return rotated.reshape(count, values.shape[1])


def swapped(value):
    return lax.ppermute(value, "head", [(0, 1), (1, 0)])


def gather_head(value):
    if lax.axis_size("head") != 2:
        return lax.all_gather(value, "head", axis=1, tiled=True)
    other = swapped(value)
    first = lax.axis_index("head") == 0
    left = jnp.where(first, value, other)
    right = jnp.where(first, other, value)
    return jnp.concatenate([left, right], axis=1)


def scatter_head(value):
    if lax.axis_size("head") != 2:
        return lax.psum_scatter(value, "head", scatter_dimension=1, tiled=True)
    place = lax.axis_index("head")
    width = value.shape[1] // 2
    theirs = lax.dynamic_slice_in_dim(value, (1 - place) * width, width, 1)
    mine = lax.dynamic_slice_in_dim(value, place * width, width, 1)
    return mine + swapped(theirs.astype(jnp.bfloat16)).astype(jnp.float32)


def sum_head(value):
    if lax.axis_size("head") != 2:
        return lax.psum(value, "head")
    return value + swapped(value)


def attend_kernel(block, q_ref, k_ref, v_ref, g_ref, cos_ref, sin_ref, out_ref, dk_acc, dv_acc):
    count = q_ref.shape[0]
    scale = 1.0 / HEAD_DIM**0.5
    dk_acc[...] = jnp.zeros_like(dk_acc)
    dv_acc[...] = jnp.zeros_like(dv_acc)

    def unrope(values, rows):
        turned = pltpu.roll(values, HEAD_DIM // 2, 1)
        return (values * cos_ref[rows, :] + turned * sin_ref[rows, :]).astype(jnp.bfloat16)

    for step in range(count // block):
        rows = slice(step * block, (step + 1) * block)
        seen = slice(0, (step + 1) * block)
        q = q_ref[rows, :]
        g = g_ref[rows, :]
        k = k_ref[seen, :]
        v = v_ref[seen, :]
        scores = lax.dot_general(q, k, LAST, preferred_element_type=jnp.float32) * scale
        q_place = step * block + lax.broadcasted_iota(jnp.int32, scores.shape, 0)
        k_place = lax.broadcasted_iota(jnp.int32, scores.shape, 1)
        scores = jnp.where(k_place <= q_place, scores, -jnp.inf)
        expo = jnp.exp(scores - jnp.max(scores, axis=-1, keepdims=True))
        prob32 = expo * (1.0 / jnp.sum(expo, axis=-1, keepdims=True))
        prob = prob32.astype(jnp.bfloat16)
        out_ref[0, rows, :] = jnp.dot(prob, v, preferred_element_type=jnp.float32).astype(
            jnp.bfloat16
        )
        dprob = lax.dot_general(g, v, LAST, preferred_element_type=jnp.float32)
        delta = jnp.sum(prob32 * dprob, axis=-1, keepdims=True)
        dscore = (prob32 * (dprob - delta) * scale).astype(jnp.bfloat16)
        out_ref[1, rows, :] = unrope(jnp.dot(dscore, k, preferred_element_type=jnp.float32), rows)
        dk_acc[seen, :] += lax.dot_general(dscore, q, FIRST, preferred_element_type=jnp.float32)
        dv_acc[seen, :] += lax.dot_general(prob, g, FIRST, preferred_element_type=jnp.float32)
    out_ref[2, :, :] = unrope(dk_acc[...], slice(0, count))
    out_ref[3, :, :] = dv_acc[...].astype(jnp.bfloat16)


def attend(query, key, value, d_context, cosine, sine):
    count = query.shape[0]
    return pl.pallas_call(
        functools.partial(attend_kernel, 256),
        out_shape=jax.ShapeDtypeStruct((4, count, HEAD_DIM), jnp.bfloat16),
        in_specs=[pl.BlockSpec(memory_space=pltpu.VMEM)] * 6,
        out_specs=pl.BlockSpec(memory_space=pltpu.VMEM),
        scratch_shapes=[
            pltpu.VMEM((count, HEAD_DIM), jnp.float32),
            pltpu.VMEM((count, HEAD_DIM), jnp.float32),
        ],
        compiler_params=pltpu.CompilerParams(vmem_limit_bytes=48 * 1024 * 1024),
        cost_estimate=pl.CostEstimate(
            flops=10 * count * count * HEAD_DIM // 2,
            bytes_accessed=16 * count * HEAD_DIM * 2,
            transcendentals=count * count // 2,
        ),
    )(query, key, value, d_context, cosine, sine)


def rolled(value, begin):
    count = value.shape[0]
    return lax.dynamic_slice_in_dim(jnp.concatenate([value, value], axis=0), begin, count, 0)


def spread_halves(packs, turn, item_cos, item_sin):
    heads, _, rows, _ = packs[0].shape
    count = lax.axis_size("ctx")
    even = lax.axis_index("ctx") % 2 == 0
    pairs = [(place, place ^ 1) for place in range(count)]
    part = rows // 2

    def swap(low, high):
        kept = jnp.where(even, low, high)
        other = lax.ppermute(jnp.where(even, high, low), "ctx", pairs)
        return jnp.where(even, kept, other), jnp.where(even, other, kept)

    def sent(packed):
        kinds = packed.shape[1]
        packed = packed.reshape(heads, kinds, 2, part, HEAD_DIM).transpose(0, 2, 1, 3, 4)
        packed = packed.reshape(count, kinds, part, HEAD_DIM)
        return lax.all_to_all(packed, "ctx", 0, 0, tiled=True)

    arrived = rolled(jnp.concatenate([sent(packed) for packed in packs], axis=1), turn)
    low, high = swap(arrived[:G_BLOCKS], arrived[G_BLOCKS:])
    mine = jnp.stack([low, high], axis=1).transpose(2, 0, 1, 3, 4)
    mine = mine.reshape(4, G_BLOCKS * rows, HEAD_DIM)
    results = attend(mine[2], mine[3], mine[0], mine[1], item_cos, item_sin)
    results = results.reshape(4, G_BLOCKS, 2, part, HEAD_DIM)
    low, high = swap(
        results[:, :, 0].transpose(1, 0, 2, 3), results[:, :, 1].transpose(1, 0, 2, 3)
    )
    both = rolled(jnp.concatenate([low, high], axis=0), (count - turn) % count)
    first, rest = both[:, :1], both[:, 1:]
    first = lax.all_to_all(first, "ctx", 0, 0, tiled=True)
    first, rest = lax.optimization_barrier((first, rest))
    rest = lax.all_to_all(rest, "ctx", 0, 0, tiled=True)

    def merged(array):
        kinds = array.shape[1]
        array = array.reshape(heads, 2, kinds, part, HEAD_DIM).transpose(1, 3, 2, 0, 4)
        return array.reshape(rows, kinds * heads * HEAD_DIM)

    return merged(first), merged(rest)


def spread_copies(packs, local_shift, start, items, item_cos, item_sin):
    packed = jnp.concatenate(packs, axis=1)
    heads, _, rows, _ = packed.shape
    count = lax.axis_size("ctx")
    groups = items // heads
    packed = jnp.broadcast_to(packed[:, None], (heads, groups, 4, rows, HEAD_DIM))
    packed = packed.reshape(items, 4, rows, HEAD_DIM)
    if items < count:
        packed = jnp.pad(packed, ((0, count - items), (0, 0), (0, 0), (0, 0)))
    arrived = lax.all_to_all(packed, "ctx", 0, 0, tiled=True)
    mine = rolled(arrived, start)[:G_BLOCKS]
    mine = mine.transpose(1, 0, 2, 3).reshape(4, G_BLOCKS * rows, HEAD_DIM)
    results = attend(mine[2], mine[3], mine[0], mine[1], item_cos, item_sin)
    results = results.reshape(4, G_BLOCKS, rows, HEAD_DIM).transpose(1, 0, 2, 3)
    back = rolled(jnp.concatenate([results] * (count // G_BLOCKS), axis=0), (count - start) % count)
    returned = lax.all_to_all(back, "ctx", 0, 0, tiled=True)
    returned = returned[:items].reshape(heads, groups, 4, rows, HEAD_DIM)
    turn = local_shift * (G_BLOCKS // 2)
    my_group = ((lax.axis_index("ctx") - turn) % count) // G_BLOCKS
    chosen = returned[:, 0]
    for other in range(1, groups):
        chosen = jnp.where((my_group == other)[:, None, None, None], returned[:, other], chosen)
    chosen = chosen.transpose(2, 1, 0, 3).reshape(rows, 4 * heads * HEAD_DIM)
    return chosen[:, : heads * HEAD_DIM], chosen[:, heads * HEAD_DIM :]


def sum_ctx(value):
    count = lax.axis_size("ctx")
    if value.size % (count * 128) != 0:
        return lax.psum(value, "ctx")
    parts = value.reshape(count, value.size // (count * 128), 128)
    part = jnp.sum(lax.all_to_all(parts, "ctx", 0, 0, tiled=True), axis=0, keepdims=True)
    whole = lax.all_to_all(jnp.broadcast_to(part, parts.shape), "ctx", 0, 0, tiled=True)
    return whole.reshape(value.shape)


def per_device(
    tokens,
    w_query,
    w_key,
    w_value,
    w_out,
    query_down,
    query_up,
    value_down,
    value_up,
    shifted,
    grad_out,
):
    rows = tokens.shape[0]
    slice_width = tokens.shape[1]
    ctx_count = lax.axis_size("ctx")
    ctx_place = lax.axis_index("ctx")
    head_place = lax.axis_index("head")
    width_local = w_query.shape[1]
    heads_local = width_local // HEAD_DIM
    seq_total = ctx_count * rows
    group = G_BLOCKS * rows
    groups = ctx_count // G_BLOCKS
    items = heads_local * groups
    assert items <= ctx_count
    half_group = G_BLOCKS // 2
    rank = query_down.shape[1]

    weights = lax.all_gather(
        jnp.concatenate([w_query, w_key, w_value, w_out.T], axis=1), "ctx", axis=0, tiled=True
    )
    w_qkv = weights[:, : 3 * width_local]
    w_out_t = weights[:, 3 * width_local :]

    full_x = gather_head(tokens)
    full_dy = gather_head(grad_out)
    local_shift = lax.dynamic_slice_in_dim(shifted, head_place * heads_local, heads_local)
    item = jnp.minimum(ctx_place, items - 1)
    item_shift = lax.dynamic_index_in_dim(local_shift, item // groups, keepdims=False)
    start = (item % groups * G_BLOCKS + item_shift * half_group) % ctx_count
    item_pos = (start * rows + jnp.arange(group, dtype=jnp.int32)) % seq_total
    item_cos, item_sin = angles(item_pos)
    item_cos = jnp.concatenate([item_cos, item_cos], axis=1)
    item_sin = jnp.concatenate([item_sin, -item_sin], axis=1)
    positions = ctx_place * rows + jnp.arange(rows, dtype=jnp.int32)
    cosine, sine = angles(positions)
    full_x, item_cos, item_sin, cosine, sine = lax.optimization_barrier(
        (full_x, item_cos, item_sin, cosine, sine)
    )
    full32 = full_x.astype(jnp.float32)
    rinv = lax.rsqrt(jnp.mean(full32 * full32, axis=-1, keepdims=True) + 1e-05)
    xn = full32 * rinv
    normed = xn.astype(jnp.bfloat16)
    low_q = jnp.dot(normed, query_down, preferred_element_type=jnp.float32).astype(jnp.bfloat16)
    low_v = jnp.dot(normed, value_down, preferred_element_type=jnp.float32).astype(jnp.bfloat16)
    v_lin = jnp.dot(
        normed, w_qkv[:, 2 * width_local :], preferred_element_type=jnp.float32
    )
    value = (v_lin + 2.0 * jnp.dot(low_v, value_up, preferred_element_type=jnp.float32)).astype(
        jnp.bfloat16
    )
    d_context = jnp.dot(full_dy, w_out_t, preferred_element_type=jnp.float32).astype(jnp.bfloat16)

    def by_head(first, second):
        pair = jnp.stack([first, second]).reshape(2, rows, heads_local, HEAD_DIM)
        return pair.transpose(2, 0, 1, 3)

    value_pair = by_head(value, d_context)
    normed_later, value_pair = lax.optimization_barrier((normed, value_pair))
    linear = jnp.dot(normed_later, w_qkv[:, : 2 * width_local], preferred_element_type=jnp.float32)
    q_lin, k_lin = jnp.split(linear, 2, axis=1)
    query = rope(
        q_lin + 2.0 * jnp.dot(low_q, query_up, preferred_element_type=jnp.float32), cosine, sine
    ).astype(jnp.bfloat16)
    key = rope(k_lin, cosine, sine).astype(jnp.bfloat16)
    packs = [value_pair, by_head(query, key)]

    if groups == 2 and items == ctx_count:
        context, grads = spread_halves(packs, item_shift * half_group, item_cos, item_sin)
    else:
        context, grads = spread_copies(packs, local_shift, start, items, item_cos, item_sin)

    partial_value = lax.dot_general(context, w_out_t, LAST, preferred_element_type=jnp.float32)
    output = (tokens.astype(jnp.float32) + scatter_head(partial_value)).astype(jnp.bfloat16)

    scale_out = 1.0 / seq_total**0.5
    dq_pre = grads[:, :width_local]
    dv_b = grads[:, 2 * width_local :]
    g_q = lax.dot_general(query_up, dq_pre, LAST, preferred_element_type=jnp.float32)
    g_v = lax.dot_general(value_up, dv_b, LAST, preferred_element_type=jnp.float32)
    g_both = 2.0 * jnp.concatenate([g_q, g_v], axis=0)
    down = jnp.dot(
        sum_head(g_both), normed.astype(jnp.float32), precision=lax.Precision.HIGHEST
    )
    up_q = 2.0 * lax.dot_general(low_q, dq_pre, FIRST, preferred_element_type=jnp.float32)
    up_v = 2.0 * lax.dot_general(low_v, dv_b, FIRST, preferred_element_type=jnp.float32)
    sums = jnp.concatenate([down, jnp.concatenate([up_q, up_v], axis=0)], axis=1)
    sums, grads = lax.optimization_barrier((sums, grads))
    total = sum_ctx(sums) * scale_out

    downs = jnp.concatenate([query_down, value_down], axis=1).astype(jnp.float32)
    d_normed = lax.dot_general(grads, w_qkv, LAST, preferred_element_type=jnp.float32)
    d_normed += lax.dot_general(
        g_both, downs, (((0,), (1,)), ((), ())), precision=lax.Precision.HIGHEST
    )
    row_mean = sum_head(jnp.sum(d_normed * xn, axis=-1, keepdims=True)) / full_x.shape[1]
    x_slice = tokens.astype(jnp.float32) * rinv
    grad_tokens = (
        grad_out.astype(jnp.float32) + rinv * (scatter_head(d_normed) - x_slice * row_mean)
    ).astype(jnp.bfloat16)

    depth = full_x.shape[1]
    downs_out = total[:, :depth].T
    ups_out = total[:, depth:]
    return (
        output,
        grad_tokens,
        downs_out[:, :rank],
        ups_out[:rank],
        downs_out[:, rank:],
        ups_out[rank:],
    )


def solution(mesh):
    in_specs = (
        P("ctx", "head"),
        P("ctx", "head"),
        P("ctx", "head"),
        P("ctx", "head"),
        P("head", "ctx"),
        P(),
        P(None, "head"),
        P(),
        P(None, "head"),
        P(),
        P("ctx", "head"),
    )
    out_specs = (P("ctx", "head"), P("ctx", "head"), P(), P(None, "head"), P(), P(None, "head"))
    return jax.shard_map(
        per_device, mesh=mesh, in_specs=in_specs, out_specs=out_specs, check_vma=False
    )
```
